32 devices in a mesh: pipe: 2 (over x), dp: 4 (over z), mp: 4 (over y, core).
Axes of the slice: x: 2, y: 2, z: 4, core: 2. Of those that a mesh axis runs over, the one named last changes fastest.
Arguments:
- layer_input: bfloat16 [2, 1024, 16384], P('pipe', 'dp', 'mp'), may hold values from -6 to 6
- kv_cotangent: bfloat16 [2, 1024, 2, 1024], P('pipe', 'dp', None, 'mp'), may hold values from -6 to 6
- kv_weight: bfloat16 [2, 16384, 2, 1024], P('pipe', 'dp', None, 'mp'), may hold values from -0.046875 to 0.046875
Outputs:
- input_grad: bfloat16 [2, 1024, 16384], P('pipe', None, ('dp', 'mp'))
- grad_mantissa: bfloat16 [2, 16384, 2, 1024], P('pipe', 'dp', None, 'mp')
- grad_scale: float32 [2, 16384, 2, 8], P('pipe', 'dp', None, 'mp')
The draws below stay inside these ranges and needn't reach their ends.
All inputs are finite; a program needn't handle non-finite values. Where the reference program divides by a largest or mean magnitude, that divisor is 1e-20 or more.
Results may differ from the reference program's by a relative error of at most 0.018.
Values may be sent and summed in bfloat16 or wider, within the bound.
No kernel may reach another device: no remote copies, remote signals or barrier semaphores. Data moves between devices by JAX's collectives and lax.ppermute only.
A program may use at most 192 MiB of HBM per device.

```python
import jax
import jax.numpy as jnp
from jax import lax

D = 16384
KVH = 8
HD = 128
BLOCK = 128
TOK_DEV = 256
TOKENS = 1024
SECTIONS = 2
N_DP = 4


def strengthened(values, key, source, target, parts, factor):
    def block_of(axis_at):
        return (jnp.arange(values.shape[axis_at]) // (values.shape[axis_at] // parts)).reshape((-1,) + (1,) * (values.ndim - 1 - axis_at))

    first = jax.random.permutation(key, parts)[block_of(target)]
    other_side = (block_of(target) + parts // 2) % parts
    return jnp.where((block_of(source) == first) | (block_of(source) == other_side), factor * values, values)


def shard_levels(own_key, shape, shards, least, high):
    gain = 1.0
    for dim, shards_of in shards:
        heights = jax.random.uniform(jax.random.fold_in(jax.random.fold_in(own_key, 6), dim), (shards_of,), jnp.float32, least / len(shards), high / len(shards))
        gain = gain * jnp.repeat(jnp.exp(heights), shape[dim] // shards_of).reshape((-1,) + (1,) * (len(shape) - 1 - dim))
    return gain


def scatter_about(rng, extent, width, bound, pieces=(), dtype=jnp.bfloat16):
    gain = shard_levels(rng, extent, pieces, -0.22, 0.18) if pieces else 1.0
    entries = jax.random.normal(rng, extent, jnp.float32) * width * gain
    return jnp.minimum(jnp.maximum(entries, -bound), bound).astype(dtype)


def bell_draw_with(rng, shape, scale, most, cuts, heavy, kind=jnp.bfloat16):
    result = scale * jax.random.normal(rng, shape, jnp.float32)
    if cuts:
        result = result * shard_levels(rng, shape, cuts, -0.22, 0.18)
    return jnp.clip(strengthened(result, jax.random.fold_in(rng, 3), *heavy), -most, most).astype(kind)


def setup_inputs(seed: int = 0) -> dict:
    key_of = jax.random.split(jax.random.key(seed), 4)
    return {
        "layer_input": bell_draw_with(key_of[0], (SECTIONS, TOKENS, D), 1.0, 6.0, ((0, 2), (1, 4), (2, 4)), (1, 2, 4, 2.0)),
        "kv_cotangent": scatter_about(key_of[1], (SECTIONS, TOKENS, 2, KVH * HD), 1.0, 6.0, ((0, 2), (1, 4), (3, 4))),
        "kv_weight": scatter_about(key_of[2], (SECTIONS, D, 2, KVH * HD), D ** -0.5, 0.046875, ((0, 2), (1, 4), (3, 4))),
    }


def one_section(section_args):
    layer_input, kv_cotangent, kv_weight = section_args
    columns = 2 * KVH * HD
    flat_grad = kv_cotangent.reshape(TOKENS, columns)
    flat_weight = kv_weight.reshape(D, columns)
    produced = lax.dot_general(flat_grad, flat_weight, (((1,), (1,)), ((), ())), preferred_element_type=jnp.float32).astype(jnp.bfloat16)
    groups_in = layer_input.reshape(N_DP, TOK_DEV, D)
    groups_grad = flat_grad.reshape(N_DP, TOK_DEV, columns)

    def group_partial(pair):
        return lax.dot_general(pair[0], pair[1], (((0,), (0,)), ((), ())), preferred_element_type=jnp.float32)

    partial_value = lax.map(group_partial, (groups_in, groups_grad))
    blocked = partial_value.reshape(N_DP, D, columns // BLOCK, BLOCK)
    grad_scale = jnp.max(jnp.abs(blocked), axis=(0, 3)) + 1e-6
    terms = (blocked / grad_scale[None, :, :, None]).astype(jnp.bfloat16)
    terms = lax.optimization_barrier(terms).astype(jnp.float32)
    grad_mantissa = jnp.sum(terms, axis=0).astype(jnp.bfloat16).reshape(D, 2, KVH * HD)
    return produced, grad_mantissa, grad_scale.reshape(D, 2, KVH * HD // BLOCK)


def reference(layer_input, kv_cotangent, kv_weight):
    produced, grad_mantissa, grad_scale = lax.map(one_section, (layer_input, kv_cotangent, kv_weight))
    input_grad = jnp.concatenate([produced[1:], jnp.zeros_like(produced[:1])], axis=0)
    return input_grad, grad_mantissa, grad_scale
```

```python
import functools

import jax
import jax.numpy as jnp
from jax import lax
from jax.experimental import pallas as pl
from jax.experimental.pallas import tpu as pltpu
from jax.sharding import PartitionSpec as P

BLOCK = 128
TILE = 256


def weight_grad_kernel(picks, *refs):
    lefts, grads_ref, mantissa_ref, scale_ref = refs[:4], refs[4], refs[-2], refs[-1]
    parts = []
    top = None
    for i, left in enumerate(lefts):
        part = jnp.dot(grads_ref[picks[i]], left[...], preferred_element_type=jnp.float32)
        parts.append(part)
        top = jnp.abs(part) if top is None else jnp.maximum(top, jnp.abs(part))
    columns, rows = top.shape
    scale = jnp.max(top.reshape(columns // BLOCK, BLOCK, rows), axis=1) + 1e-6
    scale_ref[...] = scale
    inverse = 1.0 / scale
    inverse = jnp.broadcast_to(inverse[:, None, :], (columns // BLOCK, BLOCK, rows)).reshape(columns, rows)
    total = None
    for part in parts:
        term = (part * inverse).astype(jnp.bfloat16).astype(jnp.float32)
        total = term if total is None else total + term
    mantissa_ref[...] = total.T.astype(jnp.bfloat16)


def weight_grad(picks, lefts, grads, into, first, row_total):
    columns = grads.shape[1]
    tokens, rows = lefts[0].shape
    start = first // TILE
    in_specs = [pl.BlockSpec((tokens, TILE), lambda i, picks: (0, i)) for _ in lefts]
    in_specs.append(pl.BlockSpec(grads.shape, lambda i, picks: (0, 0, 0)))
    operands = [*lefts, grads]
    aliases = {}
    if into is not None:
        for n, held in enumerate(into):
            in_specs.append(pl.BlockSpec(memory_space=pl.ANY))
            operands.append(held)
            aliases[len(operands)] = n
    return pl.pallas_call(
        weight_grad_kernel,
        grid_spec=pltpu.PrefetchScalarGridSpec(
            num_scalar_prefetch=1,
            grid=(rows // TILE,),
            in_specs=in_specs,
            out_specs=[
                pl.BlockSpec((TILE, columns), lambda i, picks: (start + i, 0)),
                pl.BlockSpec((columns // BLOCK, TILE), lambda i, picks: (0, start + i)),
            ],
        ),
        out_shape=[
            jax.ShapeDtypeStruct((row_total, columns), jnp.bfloat16),
            jax.ShapeDtypeStruct((columns // BLOCK, row_total), jnp.float32),
        ],
        input_output_aliases=aliases,
        compiler_params=pltpu.CompilerParams(vmem_limit_bytes=32 * 1024 * 1024),
        cost_estimate=pl.CostEstimate(
            flops=2 * 4 * tokens * rows * columns, bytes_accessed=2 * rows * (4 * tokens + columns), transcendentals=0
        ),
    )(picks, *operands)


def on_device(layer_input, kv_cotangent, kv_weight):
    n_pipe, n_dp, n_mp = (lax.axis_size(a) for a in ("pipe", "dp", "mp"))
    p, m = lax.axis_index("dp"), lax.axis_index("mp")
    features = layer_input[0]
    tokens, width = features.shape
    columns = 2 * kv_cotangent.shape[3]
    rows = kv_weight.shape[1]
    share = rows // n_mp

    def move(x, where):
        pairs = []
        for i in range(n_dp):
            for j in range(n_mp):
                to = where(i, j)
                if to is not None:
                    pairs.append((i * n_mp + j, to[0] * n_mp + to[1]))
        return lax.ppermute(x, ("dp", "mp"), pairs)

    def across(x):
        return move(x, lambda i, j: (i, j ^ 2))

    def other_core(x):
        return move(x, lambda i, j: (i, j ^ 1))

    own_grad = kv_cotangent[0].reshape(tokens, columns)
    grads = [own_grad] + [move(own_grad, lambda i, j, k=k: (i ^ k, j)) for k in range(1, n_dp)]

    half = width // 2
    first, second = features[:, :half], features[:, half:]

    def along(x, near, crossed):
        def where(i, j):
            q = j ^ 2 if crossed else j
            if (q // 2 == i // 2) != near:
                return None
            return (q, 2 * (j // 2) + i % 2)

        return move(x, where)

    own_side = (m // 2) == (p // 2)
    second = across(second)
    blocks = []
    for x, crossed in ((first, False), (second, True)):
        here = own_side if not crossed else jnp.logical_not(own_side)
        got = []
        for near in (False, True):
            direct = along(x, near, crossed)
            got.append(jnp.where(here, direct, across(direct)))
        far, near = got
        blocks.append((near, far, other_core(near), other_core(far)))

    quarters = kv_weight[0].reshape(n_mp, share, columns)

    def quarter(k):
        return lax.dynamic_index_in_dim(quarters, m ^ k, 0, keepdims=False)

    w = [quarter(k) for k in range(n_mp)]

    def times(g, k):
        return lax.dot_general(g, w[k], (((1,), (1,)), ((), ())), preferred_element_type=jnp.float32)

    total = jnp.zeros((n_dp * tokens, share), jnp.bfloat16)
    for k, g in enumerate(grads):
        to_other = other_core(times(g, 3).astype(jnp.bfloat16))
        to_own = other_core(times(g, 1).astype(jnp.bfloat16))
        crossing = across((times(g, 2) + to_other.astype(jnp.float32)).astype(jnp.bfloat16))
        mine = times(g, 0) + to_own.astype(jnp.float32)
        mine = (mine + crossing.astype(jnp.float32)).astype(jnp.bfloat16)
        arrived = lax.ppermute(mine, "pipe", [(i, i - 1) for i in range(1, n_pipe)])
        total = lax.dynamic_update_slice_in_dim(total, arrived, (p ^ k) * tokens, 0)

    turned = jnp.stack([g.T for g in grads])
    same = (m ^ p) & 1
    picks = jnp.stack([same, 2 + same, 1 - same, 3 - same]).astype(jnp.int32)
    into = None
    for n, four in enumerate(blocks):
        into = weight_grad(picks, four, turned, into, n * half, rows)
    mantissa, scale = into
    mantissa = mantissa.reshape(rows, 2, columns // 2)
    scale = scale.T.reshape(rows, 2, columns // (2 * BLOCK))
    return (total[None], mantissa[None], scale[None])


def solution(mesh):
    in_specs = (P("pipe", "dp", "mp"), P("pipe", "dp", None, "mp"), P("pipe", "dp", None, "mp"))
    out_specs = (
        P("pipe", None, ("dp", "mp")),
        P("pipe", "dp", None, "mp"),
        P("pipe", "dp", None, "mp"),
    )
    return jax.shard_map(on_device, mesh=mesh, in_specs=in_specs, out_specs=out_specs, check_vma=False)
```

```python
import jax
import jax.numpy as jnp
from jax import lax
from jax.experimental import pallas as pl
from jax.experimental.pallas import tpu as pltpu
from jax.sharding import PartitionSpec as P

BLOCK = 128
TILE = 512
RUNS = 2
MIB = 1024 * 1024


def weight_grad_kernel(picks, *refs):
    lefts, grads_ref = refs[:4], refs[4]
    mantissa_ref, scale_ref, turned = refs[-3:]

    @pl.when(pl.program_id(0) == 0)
    def _():
        for i in range(4):
            turned[i] = grads_ref[picks[i]].T

    top = total = None
    for i, left in enumerate(lefts):
        part = jnp.dot(turned[i], left[...], preferred_element_type=jnp.float32)
        total = part if total is None else total + part
        top = jnp.abs(part) if top is None else jnp.maximum(top, jnp.abs(part))
    columns, rows = top.shape
    blocks = columns // BLOCK
    scale = jnp.max(top.reshape(blocks, BLOCK, rows), axis=1) + 1e-6
    scale_ref[...] = scale
    inverse = 1.0 / scale
    scaled = [
        (total[b * BLOCK : (b + 1) * BLOCK] * inverse[b : b + 1]).astype(jnp.bfloat16) for b in range(blocks)
    ]
    half = blocks // 2
    mantissa_ref[:, 0, :] = jnp.concatenate(scaled[:half], axis=0).T
    mantissa_ref[:, 1, :] = jnp.concatenate(scaled[half:], axis=0).T


def weight_grad(picks, lefts, grads, into, row_total):
    columns = grads.shape[2]
    tokens, rows = lefts[0].shape
    in_specs = [pl.BlockSpec((tokens, TILE), lambda i, picks: (0, i)) for _ in lefts]
    in_specs.append(pl.BlockSpec(grads.shape, lambda i, picks: (0, 0, 0)))
    operands = [*lefts, grads]
    aliases = {}
    for n, held in enumerate(into):
        in_specs.append(pl.BlockSpec(memory_space=pl.ANY))
        operands.append(held)
        aliases[len(operands)] = n
    return pl.pallas_call(
        weight_grad_kernel,
        grid_spec=pltpu.PrefetchScalarGridSpec(
            num_scalar_prefetch=1,
            grid=(rows // TILE,),
            in_specs=in_specs,
            out_specs=[
                pl.BlockSpec((TILE, 2, columns // 2), lambda i, picks: (picks[4] + i, 0, 0)),
                pl.BlockSpec((columns // BLOCK, TILE), lambda i, picks: (0, picks[4] + i)),
            ],
            scratch_shapes=[pltpu.VMEM((4, columns, tokens), jnp.bfloat16)],
        ),
        out_shape=[
            jax.ShapeDtypeStruct((row_total, 2, columns // 2), jnp.bfloat16),
            jax.ShapeDtypeStruct((columns // BLOCK, row_total), jnp.float32),
        ],
        input_output_aliases=aliases,
        compiler_params=pltpu.CompilerParams(vmem_limit_bytes=32 * MIB),
        cost_estimate=pl.CostEstimate(
            flops=2 * 4 * tokens * rows * columns, bytes_accessed=2 * rows * (4 * tokens + columns), transcendentals=0
        ),
    )(picks, *operands)


def placed_kernel(group, *refs):
    terms, out_ref = refs[: len(refs) - 2], refs[-1]
    if len(terms) == 1:
        out_ref[...] = terms[0][...]
    else:
        out_ref[...] = (terms[0][...].astype(jnp.float32) + terms[1][...].astype(jnp.float32)).astype(jnp.bfloat16)


def first_placed_kernel(group, *refs):
    placed_kernel(group, *refs[:-1], None, refs[-1])


def placed(group, terms, into, groups):
    tokens, width = terms[0].shape
    in_specs = [pl.BlockSpec((tokens, width), lambda i, group: (0, 0)) for _ in terms]
    operands = list(terms)
    aliases = {}
    if into is not None:
        in_specs.append(pl.BlockSpec(memory_space=pl.ANY))
        operands.append(into)
        aliases[len(operands)] = 0
    return pl.pallas_call(
        placed_kernel if into is not None else first_placed_kernel,
        grid_spec=pltpu.PrefetchScalarGridSpec(
            num_scalar_prefetch=1,
            grid=(1,),
            in_specs=in_specs,
            out_specs=pl.BlockSpec((tokens, width), lambda i, group: (group[0], 0)),
        ),
        out_shape=jax.ShapeDtypeStruct((groups * tokens, width), jnp.bfloat16),
        input_output_aliases=aliases,
        cost_estimate=pl.CostEstimate(flops=tokens * width, bytes_accessed=6 * tokens * width, transcendentals=0),
    )(jnp.reshape(group, (1,)).astype(jnp.int32), *operands)


def on_device(layer_input, kv_cotangent, kv_weight):
    n_pipe, n_dp, n_mp = (lax.axis_size(a) for a in ("pipe", "dp", "mp"))
    p, m = lax.axis_index("dp"), lax.axis_index("mp")
    features = layer_input[0]
    tokens, width = features.shape
    columns = 2 * kv_cotangent.shape[3]
    rows = kv_weight.shape[1]
    share = rows // n_mp

    def move(x, where):
        pairs = []
        for s in range(n_pipe):
            for i in range(n_dp):
                for j in range(n_mp):
                    to = where(s, i, j)
                    if to is not None:
                        pairs.append(((s * n_dp + i) * n_mp + j, (to[0] * n_dp + to[1]) * n_mp + to[2]))
        return lax.ppermute(x, ("pipe", "dp", "mp"), pairs)

    def across(x):
        return move(x, lambda s, i, j: (s, i, j ^ 2))

    def other_core(x):
        return move(x, lambda s, i, j: (s, i, j ^ 1))

    def near(x):
        return move(x, lambda s, i, j: (s, 2 * (i // 2) + j % 2, 2 * (j // 2) + i % 2))

    def far(x):
        return move(x, lambda s, i, j: (s, 2 * (1 - i // 2) + j % 2, 2 * (j // 2) + i % 2))

    own_grad = kv_cotangent[0].reshape(tokens, columns)
    grads = [own_grad] + [move(own_grad, lambda s, i, j, k=k: (s, i ^ k, j)) for k in range(1, n_dp)]

    own_side = (m // 2) == (p // 2)
    half = width // 2
    run = half // RUNS
    direct, crossed = [], []
    for n in range(RUNS):
        here = features[:, n * run : (n + 1) * run]
        there = across(features[:, half + n * run : half + (n + 1) * run])
        a = near(jnp.where(own_side, here, there))
        b = far(jnp.where(own_side, there, here))
        direct.append((a, b, other_core(a), other_core(b)))
        a, b = across(a), across(b)
        crossed.append((a, b, other_core(a), other_core(b)))

    quarters = kv_weight[0].reshape(n_mp, share, columns)
    w = [lax.dynamic_index_in_dim(quarters, m ^ k, 0, keepdims=False) for k in range(n_mp)]

    def times(g, k):
        return lax.dot_general(g, w[k], (((1,), (1,)), ((), ())), preferred_element_type=jnp.float32)

    def behind(x):
        return move(x, lambda s, i, j: (s - 1, i, j) if s else None)

    total = None
    for k, g in enumerate(grads):
        to_other = other_core(times(g, 3).astype(jnp.bfloat16))
        to_own = other_core(times(g, 1).astype(jnp.bfloat16))
        for_across = (times(g, 2) + to_other.astype(jnp.float32)).astype(jnp.bfloat16)
        mine = times(g, 0) + to_own.astype(jnp.float32)
        if k < n_dp // 2:
            terms = (
                behind(mine.astype(jnp.bfloat16)),
                move(for_across, lambda s, i, j: (s - 1, i, j ^ 2) if s else None),
            )
        else:
            summed = mine + move(for_across, lambda s, i, j: (s, i, j ^ 2) if s else None).astype(jnp.float32)
            terms = (behind(summed.astype(jnp.bfloat16)),)
        total = placed(p ^ k, terms, total, n_dp)

    grads = jnp.stack(grads)
    same = (m ^ p) & 1
    out = ()
    for n in range(RUNS):
        for four, first in ((direct[n], (m // 2) != (p // 2)), (crossed[n], own_side)):
            at = (first.astype(jnp.int32) * half + n * run) // TILE
            picks = jnp.stack([same, 2 + same, 1 - same, 3 - same, at]).astype(jnp.int32)
            out = weight_grad(picks, four, grads, out, rows)
    mantissa, scale = out
    scale = scale.T.reshape(rows, 2, columns // (2 * BLOCK))
    return (total[None], mantissa[None], scale[None])


def solution(mesh):
    in_specs = (P("pipe", "dp", "mp"), P("pipe", "dp", None, "mp"), P("pipe", "dp", None, "mp"))
    out_specs = (
        P("pipe", None, ("dp", "mp")),
        P("pipe", "dp", None, "mp"),
        P("pipe", "dp", None, "mp"),
    )
    return jax.shard_map(on_device, mesh=mesh, in_specs=in_specs, out_specs=out_specs, check_vma=False)
```

```python
import jax
import jax.numpy as jnp
from jax import lax
from jax.experimental import pallas as pl
from jax.experimental.pallas import tpu as pltpu
from jax.sharding import PartitionSpec as P

BLOCK = 128
TILE = 256
RUNS = 2
MIB = 1024 * 1024
LIGHT = pl.CostEstimate(flops=0, bytes_accessed=0, transcendentals=0)


def turned_kernel(slots, *refs):
    for k in range(4):
        refs[-1][slots[k]] = refs[k // 2][k % 2].T


def turned(slots, grads):
    groups, tokens, columns = grads[0].shape
    return pl.pallas_call(
        turned_kernel,
        grid_spec=pltpu.PrefetchScalarGridSpec(
            num_scalar_prefetch=1,
            grid=(1,),
            in_specs=[pl.BlockSpec((groups, tokens, columns), lambda i, slots: (0, 0, 0)) for _ in grads],
            out_specs=pl.BlockSpec((2 * groups, columns, tokens), lambda i, slots: (0, 0, 0)),
        ),
        out_shape=jax.ShapeDtypeStruct((2 * groups, columns, tokens), jnp.bfloat16),
        cost_estimate=LIGHT,
    )(slots, *grads)


def stacked_kernel(a_ref, b_ref, out_ref):
    out_ref[0] = a_ref[...]
    out_ref[1] = b_ref[...]


def stacked(a, b):
    return pl.pallas_call(
        stacked_kernel, out_shape=jax.ShapeDtypeStruct((2, *a.shape), a.dtype), cost_estimate=LIGHT
    )(a, b)


def across_dot(a, b):
    return lax.dot_general(a, b, (((1,), (1,)), ((), ())), preferred_element_type=jnp.float32)


def input_grad_kernel(m, *refs):
    groups = (len(refs) - 6) // 2
    owns, others = refs[:groups], refs[groups : 2 * groups]
    own2_ref, own0_ref, other2_ref, other0_ref, a_ref, m_ref = refs[2 * groups :]
    for n in range(groups):
        own, other = owns[n][...], others[n][...]
        a = across_dot(own, own2_ref[...]) + across_dot(other, other2_ref[...])
        a_ref[n] = a.astype(a_ref.dtype)
        b = across_dot(own, own0_ref[...]) + across_dot(other, other0_ref[...])
        m_ref[n] = b.astype(m_ref.dtype)


def input_grad(m, owns, others, weights, other_weights, parts, kept):
    tokens, columns = owns[0].shape
    groups = len(owns)
    share = weights.shape[0] // parts
    tile = share // 2
    in_specs = [pl.BlockSpec((tokens, columns), lambda i, m: (0, 0)) for _ in range(2 * groups)]
    in_specs += [pl.BlockSpec((tile, columns), lambda i, m, k=k: ((m[0] ^ k) * 2 + i, 0)) for k in (2, 0, 2, 0)]
    out = pl.BlockSpec((groups, tokens, tile), lambda i, m: (0, 0, i))
    return pl.pallas_call(
        input_grad_kernel,
        grid_spec=pltpu.PrefetchScalarGridSpec(
            num_scalar_prefetch=1, grid=(share // tile,), in_specs=in_specs, out_specs=[out, out]
        ),
        out_shape=[jax.ShapeDtypeStruct((groups, tokens, share), t) for t in (jnp.bfloat16, kept)],
        compiler_params=pltpu.CompilerParams(vmem_limit_bytes=32 * MIB),
        cost_estimate=LIGHT,
    )(jnp.reshape(m, (1,)).astype(jnp.int32), *owns, *others, weights, weights, other_weights, other_weights)


def chosen_kernel(flag, here_ref, there_ref, a_ref, b_ref):
    @pl.when(flag[0] == 1)
    def _():
        a_ref[...] = here_ref[...]
        b_ref[...] = there_ref[...]

    @pl.when(flag[0] == 0)
    def _():
        a_ref[...] = there_ref[...]
        b_ref[...] = here_ref[...]


def chosen(flag, here, there, n, runs):
    tokens, width = there.shape
    run = width // runs
    block = (tokens // 2, run)
    return pl.pallas_call(
        chosen_kernel,
        grid_spec=pltpu.PrefetchScalarGridSpec(
            num_scalar_prefetch=1,
            grid=(2,),
            in_specs=[pl.BlockSpec(block, lambda i, flag: (i, n))] * 2,
            out_specs=[pl.BlockSpec(block, lambda i, flag: (i, 0))] * 2,
        ),
        out_shape=[jax.ShapeDtypeStruct((tokens, run), here.dtype)] * 2,
        cost_estimate=LIGHT,
    )(jnp.reshape(flag, (1,)).astype(jnp.int32), here, there)


def summed_kernel(a_ref, b_ref, out_ref):
    out_ref[...] = (a_ref[...].astype(jnp.float32) + b_ref[...].astype(jnp.float32)).astype(out_ref.dtype)


def summed(a, b):
    block = pl.BlockSpec((1, *a.shape[1:]), lambda i: (i, 0, 0))
    return pl.pallas_call(
        summed_kernel,
        grid=(a.shape[0],),
        in_specs=[block, block],
        out_specs=block,
        out_shape=jax.ShapeDtypeStruct(a.shape, jnp.bfloat16),
        cost_estimate=LIGHT,
    )(a, b)


def weight_grad_kernel(at, *refs):
    lefts, grads_ref = refs[:4], refs[4]
    mantissa_ref, scale_ref = refs[-2:]
    top = total = None
    for i, left in enumerate(lefts):
        part = jnp.dot(grads_ref[i], left[...], preferred_element_type=jnp.float32)
        total = part if total is None else total + part
        top = jnp.abs(part) if top is None else jnp.maximum(top, jnp.abs(part))
    columns, rows = top.shape
    blocks = columns // BLOCK
    scale = jnp.max(top.reshape(blocks, BLOCK, rows), axis=1) + 1e-6
    scale_ref[...] = scale
    inverse = 1.0 / scale
    scaled = [
        (total[b * BLOCK : (b + 1) * BLOCK] * inverse[b : b + 1]).astype(jnp.bfloat16) for b in range(blocks)
    ]
    half = blocks // 2
    mantissa_ref[:, 0, :] = jnp.concatenate(scaled[:half], axis=0).T
    mantissa_ref[:, 1, :] = jnp.concatenate(scaled[half:], axis=0).T


def weight_grad(at, lefts, grads, into, row_total):
    columns = grads.shape[1]
    tokens, rows = lefts[0].shape
    in_specs = [pl.BlockSpec((tokens, TILE), lambda i, at: (0, i)) for _ in lefts]
    in_specs.append(pl.BlockSpec(grads.shape, lambda i, at: (0, 0, 0)))
    operands = [*lefts, grads]
    aliases = {}
    for n, held in enumerate(into):
        in_specs.append(pl.BlockSpec(memory_space=pl.ANY))
        operands.append(held)
        aliases[len(operands)] = n
    return pl.pallas_call(
        weight_grad_kernel,
        grid_spec=pltpu.PrefetchScalarGridSpec(
            num_scalar_prefetch=1,
            grid=(rows // TILE,),
            in_specs=in_specs,
            out_specs=[
                pl.BlockSpec((TILE, 2, columns // 2), lambda i, at: (at[0] + i, 0, 0)),
                pl.BlockSpec((columns // BLOCK, TILE), lambda i, at: (0, at[0] + i)),
            ],
        ),
        out_shape=[
            jax.ShapeDtypeStruct((row_total, 2, columns // 2), jnp.bfloat16),
            jax.ShapeDtypeStruct((columns // BLOCK, row_total), jnp.float32),
        ],
        input_output_aliases=aliases,
        compiler_params=pltpu.CompilerParams(vmem_limit_bytes=32 * MIB),
        cost_estimate=LIGHT,
    )(at, *operands)


def placed_kernel(group, *refs):
    terms, out_ref = refs[:-1], refs[-1]
    if len(terms) == 1:
        out_ref[...] = terms[0][0]
    else:
        out_ref[...] = (terms[0][0].astype(jnp.float32) + terms[1][0].astype(jnp.float32)).astype(jnp.bfloat16)


def placed_again_kernel(group, *refs):
    placed_kernel(group, *refs[:-2], refs[-1])


def placed(group, first, by, terms, into, groups):
    some, tokens, width = terms[0].shape
    in_specs = [pl.BlockSpec((1, tokens, width), lambda i, group: (i, 0, 0)) for _ in terms]
    operands = list(terms)
    aliases = {}
    if into is not None:
        in_specs.append(pl.BlockSpec(memory_space=pl.ANY))
        operands.append(into)
        aliases[len(operands)] = 0
    return pl.pallas_call(
        placed_kernel if into is None else placed_again_kernel,
        grid_spec=pltpu.PrefetchScalarGridSpec(
            num_scalar_prefetch=1,
            grid=(some,),
            in_specs=in_specs,
            out_specs=pl.BlockSpec((tokens, width), lambda i, group: (group[0] ^ (first + by * i), 0)),
        ),
        out_shape=jax.ShapeDtypeStruct((groups * tokens, width), jnp.bfloat16),
        input_output_aliases=aliases,
        cost_estimate=LIGHT,
    )(jnp.reshape(group, (1,)).astype(jnp.int32), *operands)


def on_device(layer_input, kv_cotangent, kv_weight):
    n_pipe, n_dp, n_mp = (lax.axis_size(a) for a in ("pipe", "dp", "mp"))
    p, m = lax.axis_index("dp"), lax.axis_index("mp")
    features = layer_input[0]
    tokens, width = features.shape
    columns = 2 * kv_cotangent.shape[3]
    rows = kv_weight.shape[1]
    share = rows // n_mp

    def move(x, where):
        pairs = []
        for s in range(n_pipe):
            for i in range(n_dp):
                for j in range(n_mp):
                    to = where(s, i, j)
                    if to is not None:
                        pairs.append(((s * n_dp + i) * n_mp + j, (to[0] * n_dp + to[1]) * n_mp + to[2]))
        return lax.ppermute(x, ("pipe", "dp", "mp"), pairs)

    def across(x):
        return move(x, lambda s, i, j: (s, i, j ^ 2))

    def other_core(x):
        return move(x, lambda s, i, j: (s, i, j ^ 1))

    def near(x):
        return move(x, lambda s, i, j: (s, 2 * (i // 2) + j % 2, 2 * (j // 2) + i % 2))

    def far(x):
        return move(x, lambda s, i, j: (s, 2 * (1 - i // 2) + j % 2, 2 * (j // 2) + i % 2))

    def across(x):
        return move(x, lambda s, i, j: (s, i, j ^ 2))

    def behind(x):
        return move(x, lambda s, i, j: (s - 1, i, j) if s else None)

    def behind_across(x):
        return move(x, lambda s, i, j: (s - 1, i, j ^ 2) if s else None)

    def across_but_first(x):
        return move(x, lambda s, i, j: (s, i, j ^ 2) if s else None)

    last = []

    def step(x):
        x = lax.optimization_barrier((x, *last))[0] if last else x
        last[:] = [x]
        return x

    def now(x):
        return lax.optimization_barrier((x, *last))[0] if last else x

    same = (m ^ p) & 1
    slots = jnp.where(same == 0, jnp.array([0, 1, 2, 3], jnp.int32), jnp.array([2, 3, 0, 1], jnp.int32))
    own_side = (m // 2) == (p // 2)
    half = width // 2
    run = half // RUNS
    direct_at = (jnp.where(own_side, 0, half) // TILE).astype(jnp.int32)
    crossed_at = (jnp.where(own_side, half, 0) // TILE).astype(jnp.int32)

    def weighed(at, n, four, into):
        return weight_grad(jnp.reshape(at + n * run // TILE, (1,)), four, turned_grads, into, rows)

    there = across(features[:, half:])
    g0 = kv_cotangent[0].reshape(tokens, columns)
    g2 = move(g0, lambda s, i, j: (s, i ^ 2, j))
    g0_core = other_core(g0)
    other_weights = other_core(kv_weight)
    weights = kv_weight[0].reshape(rows, columns)
    other_weights = step(other_weights)[0].reshape(rows, columns)
    g2 = step(g2)
    g02 = stacked(g0, g2)
    last[:] = [g02]
    g13 = move(g02, lambda s, i, j: (s, i ^ 1, j))
    g2_core = other_core(now(g2))

    g0_core = step(g0_core)
    g2_core = step(g2_core)
    a_late, m_late = input_grad(m, (g0, g2), (g0_core, g2_core), weights, other_weights, n_mp, jnp.bfloat16)
    last[:] = [a_late]
    late_own = behind(m_late)
    there = step(there)
    a, b = chosen(own_side, features, there, 0, RUNS)
    last[:] = [a]
    far0 = far(b)
    near0 = near(a)
    a, b = chosen(own_side, features, now(there), 1, RUNS)
    last[:] = [a]
    g13 = step(g13)
    g1, g3 = g13[0], g13[1]
    g1_core, g3_core = other_core(g1), other_core(g3)
    turned_grads = turned(slots, (g02, g13))
    last[:] = [turned_grads]
    g1_core = step(g1_core)
    g3_core = step(g3_core)
    a_early, m_early = input_grad(m, (g1, g3), (g1_core, g3_core), weights, other_weights, n_mp, jnp.float32)
    last[:] = [a_early]
    a_across = across_but_first(a_early)
    near0 = step(near0)
    near0_across = across(near0)
    far0 = step(far0)
    far0_across = across(far0)
    far1 = far(now(b))
    near1 = near(now(a))
    near0_core, far0_core = other_core(now(near0)), other_core(now(far0))
    late_own = step(late_own)
    late_across = behind_across(now(a_late))
    near0_core, far0_core = step(near0_core), step(far0_core)
    out = weighed(direct_at, 0, (near0, far0, near0_core, far0_core), ())
    last[:] = [out[0]]
    a_across = step(a_across)
    early_sum = summed(m_early, a_across)
    last[:] = [early_sum]
    early = behind(early_sum)
    near1 = step(near1)
    near1_across = across(near1)
    far1 = step(far1)
    far1_across = across(far1)
    near1_core, far1_core = other_core(now(near1)), other_core(now(far1))
    near0_across = step(near0_across)
    far0_across = step(far0_across)
    near0_across_core, far0_across_core = other_core(now(near0_across)), other_core(now(far0_across))
    near1_core, far1_core = step(near1_core), step(far1_core)
    out = weighed(direct_at, 1, (near1, far1, near1_core, far1_core), out)
    last[:] = [out[0]]
    near0_across_core, far0_across_core = step(near0_across_core), step(far0_across_core)
    out = weighed(crossed_at, 0, (near0_across, far0_across, near0_across_core, far0_across_core), out)
    last[:] = [out[0]]
    late_across = step(late_across)
    total = placed(p, 0, 2, (late_own, late_across), None, n_dp)
    last[:] = [total]
    near1_across = step(near1_across)
    near1_across_core = other_core(now(near1_across))
    early = step(early)
    total = placed(p, 1, 2, (early,), total, n_dp)
    last[:] = [total]
    far1_across = step(far1_across)
    far1_across_core = other_core(far1_across)
    near1_across_core, far1_across_core = step(near1_across_core), step(far1_across_core)
    out = weighed(crossed_at, 1, (near1_across, far1_across, near1_across_core, far1_across_core), out)
    mantissa, scale = out
    scale = scale.T.reshape(rows, 2, columns // (2 * BLOCK))
    return (total[None], mantissa[None], scale[None])


def solution(mesh):
    in_specs = (P("pipe", "dp", "mp"), P("pipe", "dp", None, "mp"), P("pipe", "dp", None, "mp"))
    out_specs = (
        P("pipe", None, ("dp", "mp")),
        P("pipe", "dp", None, "mp"),
        P("pipe", "dp", None, "mp"),
    )
    return jax.shard_map(on_device, mesh=mesh, in_specs=in_specs, out_specs=out_specs, check_vma=False)
```

```python
import jax
import jax.numpy as jnp
from jax import lax
from jax.experimental import pallas as pl
from jax.experimental.pallas import tpu as pltpu
from jax.sharding import PartitionSpec as P

BLOCK = 128
TILE = 512
MIB = 1024 * 1024
VMEM_MIB = 60
PARAMS = pltpu.CompilerParams(vmem_limit_bytes=VMEM_MIB * MIB)
LIGHT = pl.CostEstimate(flops=0, bytes_accessed=0, transcendentals=0)


def turned_kernel(slots, *refs):
    for k, ref in enumerate(refs[:-1]):
        refs[-1][slots[k]] = ref[...].T


def turned(slots, grads):
    tokens, columns = grads[0].shape
    return pl.pallas_call(
        turned_kernel,
        grid_spec=pltpu.PrefetchScalarGridSpec(
            num_scalar_prefetch=1,
            grid=(1,),
            in_specs=[pl.BlockSpec((tokens, columns), lambda i, slots: (0, 0)) for _ in grads],
            out_specs=pl.BlockSpec((4, columns, tokens), lambda i, slots: (0, 0, 0)),
        ),
        out_shape=jax.ShapeDtypeStruct((4, columns, tokens), jnp.bfloat16),
        compiler_params=PARAMS,
        cost_estimate=LIGHT,
    )(slots, *grads)


def across_dot(a, b):
    return lax.dot_general(a, b, (((1,), (1,)), ((), ())), preferred_element_type=jnp.float32)


def input_grad_kernel(m, *refs):
    groups = (len(refs) - 6) // 2
    owns, others = refs[:groups], refs[groups : 2 * groups]
    own2_ref, own0_ref, other2_ref, other0_ref, a_ref, m_ref = refs[2 * groups :]
    for n in range(groups):
        own, other = owns[n][...], others[n][...]
        a = across_dot(own, own2_ref[...]) + across_dot(other, other2_ref[...])
        a_ref[n] = a.astype(a_ref.dtype)
        b = across_dot(own, own0_ref[...]) + across_dot(other, other0_ref[...])
        m_ref[n] = b.astype(m_ref.dtype)


def input_grad(m, owns, others, weights, other_weights, parts, kept):
    tokens, columns = owns[0].shape
    groups = len(owns)
    share = weights.shape[0] // parts
    tile = share // 2
    in_specs = [pl.BlockSpec((tokens, columns), lambda i, m: (0, 0)) for _ in range(2 * groups)]
    in_specs += [pl.BlockSpec((tile, columns), lambda i, m, k=k: ((m[0] ^ k) * 2 + i, 0)) for k in (2, 0, 2, 0)]
    out = pl.BlockSpec((groups, tokens, tile), lambda i, m: (0, 0, i))
    return pl.pallas_call(
        input_grad_kernel,
        grid_spec=pltpu.PrefetchScalarGridSpec(
            num_scalar_prefetch=1, grid=(share // tile,), in_specs=in_specs, out_specs=[out, out]
        ),
        out_shape=[jax.ShapeDtypeStruct((groups, tokens, share), t) for t in (jnp.bfloat16, kept)],
        compiler_params=PARAMS,
        cost_estimate=LIGHT,
    )(jnp.reshape(m, (1,)).astype(jnp.int32), *owns, *others, weights, weights, other_weights, other_weights)


def chosen_kernel(flag, here_ref, there_ref, a_ref, b_ref):
    @pl.when(flag[0] == 1)
    def _():
        a_ref[...] = here_ref[...]
        b_ref[...] = there_ref[...]

    @pl.when(flag[0] == 0)
    def _():
        a_ref[...] = there_ref[...]
        b_ref[...] = here_ref[...]


def chosen(flag, run, here, there, runs):
    tokens, width = there.shape
    width = width // runs
    block = (tokens // 2, width)
    return pl.pallas_call(
        chosen_kernel,
        grid_spec=pltpu.PrefetchScalarGridSpec(
            num_scalar_prefetch=1,
            grid=(2,),
            in_specs=[pl.BlockSpec(block, lambda i, flag: (i, flag[1]))] * 2,
            out_specs=[pl.BlockSpec(block, lambda i, flag: (i, 0))] * 2,
        ),
        out_shape=[jax.ShapeDtypeStruct((tokens, width), here.dtype)] * 2,
        compiler_params=PARAMS,
        cost_estimate=LIGHT,
    )(jnp.stack([flag.astype(jnp.int32), run.astype(jnp.int32)]), here, there)


def summed_kernel(a_ref, b_ref, out_ref):
    out_ref[...] = (a_ref[...].astype(jnp.float32) + b_ref[...].astype(jnp.float32)).astype(out_ref.dtype)


def summed(a, b):
    block = pl.BlockSpec((1, *a.shape[1:]), lambda i: (i, 0, 0))
    return pl.pallas_call(
        summed_kernel,
        grid=(a.shape[0],),
        in_specs=[block, block],
        out_specs=block,
        out_shape=jax.ShapeDtypeStruct(a.shape, jnp.bfloat16),
        compiler_params=PARAMS,
        cost_estimate=LIGHT,
    )(a, b)


def weight_grad_kernel(at, *refs):
    lefts, grads_ref = refs[:4], refs[4]
    mantissa_ref, scale_ref = refs[-2:]
    top = total = None
    for i, left in enumerate(lefts):
        part = jnp.dot(grads_ref[i], left[...], preferred_element_type=jnp.float32)
        total = part if total is None else total + part
        top = jnp.abs(part) if top is None else jnp.maximum(top, jnp.abs(part))
    columns, rows = top.shape
    blocks = columns // BLOCK
    scale = jnp.max(top.reshape(blocks, BLOCK, rows), axis=1) + 1e-6
    for k in range(2):
        scale_ref[k] = scale[k * (blocks // 2) : (k + 1) * (blocks // 2)]
    inverse = 1.0 / scale
    scaled = [
        (total[b * BLOCK : (b + 1) * BLOCK] * inverse[b : b + 1]).astype(jnp.bfloat16) for b in range(blocks)
    ]
    half = blocks // 2
    mantissa_ref[:, 0, :] = jnp.concatenate(scaled[:half], axis=0).T
    mantissa_ref[:, 1, :] = jnp.concatenate(scaled[half:], axis=0).T


def weight_grad(at, lefts, grads, into, row_total):
    columns = grads.shape[1]
    tokens, rows = lefts[0].shape
    in_specs = [pl.BlockSpec((tokens, TILE), lambda i, at: (0, i)) for _ in lefts]
    in_specs.append(pl.BlockSpec(grads.shape, lambda i, at: (0, 0, 0)))
    operands = [*lefts, grads]
    aliases = {}
    for n, held in enumerate(into):
        in_specs.append(pl.BlockSpec(memory_space=pl.ANY))
        operands.append(held)
        aliases[len(operands)] = n
    return pl.pallas_call(
        weight_grad_kernel,
        grid_spec=pltpu.PrefetchScalarGridSpec(
            num_scalar_prefetch=1,
            grid=(rows // TILE,),
            in_specs=in_specs,
            out_specs=[
                pl.BlockSpec((TILE, 2, columns // 2), lambda i, at: (at[0] + i, 0, 0)),
                pl.BlockSpec((2, columns // BLOCK // 2, TILE), lambda i, at: (0, 0, at[0] + i)),
            ],
        ),
        out_shape=[
            jax.ShapeDtypeStruct((row_total, 2, columns // 2), jnp.bfloat16),
            jax.ShapeDtypeStruct((2, columns // BLOCK // 2, row_total), jnp.float32),
        ],
        input_output_aliases=aliases,
        compiler_params=PARAMS,
        cost_estimate=LIGHT,
    )(at, *operands)


def rows_placed_kernel(at, mantissa_ref, scale_ref, held_m, held_s, out_m_ref, out_s_ref):
    out_m_ref[...] = mantissa_ref[...]
    out_s_ref[...] = scale_ref[...]


def rows_placed(at, part, into):
    mantissa, scale = part
    rows, pair, columns = mantissa.shape
    tile = TILE
    blocks = scale.shape[1]
    return pl.pallas_call(
        rows_placed_kernel,
        grid_spec=pltpu.PrefetchScalarGridSpec(
            num_scalar_prefetch=1,
            grid=(rows // tile,),
            in_specs=[
                pl.BlockSpec((tile, pair, columns), lambda i, at: (i, 0, 0)),
                pl.BlockSpec((2, blocks, tile), lambda i, at: (0, 0, i)),
                pl.BlockSpec(memory_space=pl.ANY),
                pl.BlockSpec(memory_space=pl.ANY),
            ],
            out_specs=[
                pl.BlockSpec((tile, pair, columns), lambda i, at: (at[0] + i, 0, 0)),
                pl.BlockSpec((2, blocks, tile), lambda i, at: (0, 0, at[0] + i)),
            ],
        ),
        out_shape=[jax.ShapeDtypeStruct(held.shape, held.dtype) for held in into],
        input_output_aliases={3: 0, 4: 1},
        compiler_params=PARAMS,
        cost_estimate=LIGHT,
    )(at, mantissa, scale, *into)


def placed_kernel(group, *refs):
    terms, out_ref = refs[:-1], refs[-1]
    if len(terms) == 1:
        out_ref[...] = terms[0][0]
    else:
        out_ref[...] = (terms[0][0].astype(jnp.float32) + terms[1][0].astype(jnp.float32)).astype(jnp.bfloat16)


def placed_again_kernel(group, *refs):
    placed_kernel(group, *refs[:-2], refs[-1])


def placed(group, first, terms, into, groups):
    some, tokens, width = terms[0].shape
    in_specs = [pl.BlockSpec((1, tokens, width), lambda i, group: (i, 0, 0)) for _ in terms]
    operands = list(terms)
    aliases = {}
    if into is not None:
        in_specs.append(pl.BlockSpec(memory_space=pl.ANY))
        operands.append(into)
        aliases[len(operands)] = 0
    return pl.pallas_call(
        placed_kernel if into is None else placed_again_kernel,
        grid_spec=pltpu.PrefetchScalarGridSpec(
            num_scalar_prefetch=1,
            grid=(some,),
            in_specs=in_specs,
            out_specs=pl.BlockSpec((tokens, width), lambda i, group: (group[0] ^ (first + i), 0)),
        ),
        out_shape=jax.ShapeDtypeStruct((groups * tokens, width), jnp.bfloat16),
        input_output_aliases=aliases,
        compiler_params=PARAMS,
        cost_estimate=LIGHT,
    )(jnp.reshape(group, (1,)).astype(jnp.int32), *operands)


def on_device(layer_input, kv_cotangent, kv_weight):
    n_pipe, n_dp, n_mp = (lax.axis_size(a) for a in ("pipe", "dp", "mp"))
    p, m = lax.axis_index("dp"), lax.axis_index("mp")
    features = layer_input[0]
    tokens, width = features.shape
    columns = 2 * kv_cotangent.shape[3]
    rows = kv_weight.shape[1]
    share = rows // n_mp

    def move(x, where):
        pairs = []
        for s in range(n_pipe):
            for i in range(n_dp):
                for j in range(n_mp):
                    to = where(s, i, j)
                    if to is not None:
                        pairs.append(((s * n_dp + i) * n_mp + j, (to[0] * n_dp + to[1]) * n_mp + to[2]))
        return lax.ppermute(x, ("pipe", "dp", "mp"), pairs)

    def across(x):
        return move(x, lambda s, i, j: (s, i, j ^ 2))

    def other_core(x):
        return move(x, lambda s, i, j: (s, i, j ^ 1))

    def near(x, other):
        return move(x, lambda s, i, j: (s, 2 * (i // 2) + j % 2, 2 * (j // 2) + (i + other) % 2))

    def far(x, other):
        return move(x, lambda s, i, j: (s, 2 * (1 - i // 2) + j % 2, 2 * (j // 2) + (i + other) % 2))

    def across(x):
        return move(x, lambda s, i, j: (s, i, j ^ 2))

    def behind(x):
        return move(x, lambda s, i, j: (s - 1, i, j) if s else None)

    def behind_across(x):
        return move(x, lambda s, i, j: (s - 1, i, j ^ 2) if s else None)

    def across_but_first(x):
        return move(x, lambda s, i, j: (s, i, j ^ 2) if s else None)

    same = (m ^ p) & 1
    slots = jnp.where(same == 0, jnp.array([0, 1, 2, 3], jnp.int32), jnp.array([1, 0, 3, 2], jnp.int32))
    own_side = (m // 2) == (p // 2)
    half = width // 2
    run = half // 2
    core = m & 1
    direct_at = jnp.where(own_side, 0, half)
    crossed_at = jnp.where(own_side, half, 0)

    def tile_at(first):
        return jnp.reshape(first // TILE, (1,)).astype(jnp.int32)

    last = []

    def now(x):
        return lax.optimization_barrier((x, *last))[0] if last else x

    def ran(x):
        last[:] = [x]

    def step(x):
        x = now(x)
        ran(x)
        return x

    def group(k, x):
        return move(x, lambda s, i, j: (s, i ^ k, j))

    g0 = kv_cotangent[0].reshape(tokens, columns)
    own_w = step(kv_weight[0].reshape(rows, columns))
    other_raw = step(other_core(kv_weight))
    g0_core = step(other_core(g0))
    other_w = step(other_raw[0].reshape(rows, columns))
    g1 = step(group(1, g0))
    g2 = step(group(2, g0))
    g1_core = step(other_core(g1))
    a_early, m_early = input_grad(
        m, (now(g0), g1), (g0_core, g1_core), own_w, other_w, n_mp, jnp.float32
    )
    ran(a_early)
    there = step(across(features[:, half:]))
    near0_sent, far0_sent = chosen(own_side, p & 1, features, now(there), 2)
    ran(near0_sent)
    g3 = step(group(3, g0))
    near1_sent, far1_sent = chosen(own_side, (p + 1) & 1, features, now(there), 2)
    ran(near1_sent)
    g2_core = step(other_core(g2))
    near1_begun = near(now(near1_sent), 1)
    g3_core = step(other_core(g3))
    a_late, m_late = input_grad(
        m, (now(g2), g3), (g2_core, g3_core), own_w, other_w, n_mp, jnp.bfloat16
    )
    ran(a_late)
    far1_begun = far(now(far1_sent), 1)
    near0 = step(near(near0_sent, 0))
    near1 = step(near1_begun)
    near1_x_begun = across(now(near1))
    a_across = step(across_but_first(a_early))
    early_sum = step(summed(now(m_early), a_across))
    far0 = step(far(far0_sent, 0))
    other_turned = step(turned(slots, (now(g0_core), g1_core, g2_core, g3_core)))
    late_across_begun = behind_across(now(a_late))
    late_own = step(behind(m_late))
    own_turned = step(turned(slots, (now(g0), g1, g2, g3)))
    near0_x = step(across(near0))
    near1_x = step(near1_x_begun)
    far1 = step(far1_begun)
    far1_x_begun = across(now(far1))
    direct_m_sent, direct_s_sent = weight_grad(tile_at(0), (now(near0), near1, far0, far1), other_turned, (), run)
    ran(direct_m_sent)
    early_begun = behind(now(early_sum))
    out = weight_grad(tile_at(direct_at + core * run), (now(near0), near1, far0, far1), own_turned, (), rows)
    ran(out[0])
    far0_x = step(across(far0))
    late_across = step(late_across_begun)
    total = step(placed(p, 2, (now(late_own), late_across), None, n_dp))
    far1_x = step(far1_x_begun)
    crossed_m_sent, crossed_s_sent = weight_grad(tile_at(0), (now(near0_x), near1_x, far0_x, far1_x), other_turned, (), run)
    ran(crossed_m_sent)
    out = weight_grad(tile_at(crossed_at + core * run), (now(near0_x), near1_x, far0_x, far1_x), own_turned, out, rows)
    ran(out[0])
    direct_m = step(other_core(direct_m_sent))
    direct_s = step(other_core(direct_s_sent))
    out = rows_placed(tile_at(direct_at + (1 - core) * run), (now(direct_m), direct_s), out)
    ran(out[0])
    early = step(early_begun)
    total = step(placed(p, 0, (now(early),), total, n_dp))
    crossed_m = step(other_core(crossed_m_sent))
    crossed_s = step(other_core(crossed_s_sent))
    out = rows_placed(tile_at(crossed_at + (1 - core) * run), (now(crossed_m), crossed_s), out)
    ran(out[0])
    mantissa, scale = out
    scale = scale.transpose(2, 0, 1)
    return (total[None], mantissa[None], scale[None])


def solution(mesh):
    in_specs = (P("pipe", "dp", "mp"), P("pipe", "dp", None, "mp"), P("pipe", "dp", None, "mp"))
    out_specs = (
        P("pipe", None, ("dp", "mp")),
        P("pipe", "dp", None, "mp"),
        P("pipe", "dp", None, "mp"),
    )
    return jax.shard_map(on_device, mesh=mesh, in_specs=in_specs, out_specs=out_specs, check_vma=False)
```

```python
import jax
import jax.numpy as jnp
from jax import lax
from jax.experimental import pallas as pl
from jax.experimental.pallas import tpu as pltpu
from jax.sharding import PartitionSpec as P

BLOCK = 128
TILE = 512
MIB = 1024 * 1024
VMEM_MIB = 60
PARAMS = pltpu.CompilerParams(vmem_limit_bytes=VMEM_MIB * MIB)
LIGHT = pl.CostEstimate(flops=0, bytes_accessed=0, transcendentals=0)


def turned_kernel(slots, *refs):
    for k, ref in enumerate(refs[:-1]):
        refs[-1][slots[k]] = ref[...].T


def turned(slots, grads):
    tokens, columns = grads[0].shape
    return pl.pallas_call(
        turned_kernel,
        grid_spec=pltpu.PrefetchScalarGridSpec(
            num_scalar_prefetch=1,
            grid=(1,),
            in_specs=[pl.BlockSpec((tokens, columns), lambda i, slots: (0, 0)) for _ in grads],
            out_specs=pl.BlockSpec((4, columns, tokens), lambda i, slots: (0, 0, 0)),
        ),
        out_shape=jax.ShapeDtypeStruct((4, columns, tokens), jnp.bfloat16),
        compiler_params=PARAMS,
        cost_estimate=LIGHT,
    )(slots, *grads)


def across_dot(a, b):
    return lax.dot_general(a, b, (((1,), (1,)), ((), ())), preferred_element_type=jnp.float32)


def input_grad_kernel(m, *refs):
    groups = (len(refs) - 6) // 2
    owns, others = refs[:groups], refs[groups : 2 * groups]
    own2_ref, own0_ref, other2_ref, other0_ref, a_ref, m_ref = refs[2 * groups :]
    for n in range(groups):
        own, other = owns[n][...], others[n][...]
        a = across_dot(own, own2_ref[...]) + across_dot(other, other2_ref[...])
        a_ref[n] = a.astype(a_ref.dtype)
        b = across_dot(own, own0_ref[...]) + across_dot(other, other0_ref[...])
        m_ref[n] = b.astype(m_ref.dtype)


def input_grad(m, owns, others, weights, other_weights, parts, kept):
    tokens, columns = owns[0].shape
    groups = len(owns)
    share = weights.shape[0] // parts
    tile = share // 2
    in_specs = [pl.BlockSpec((tokens, columns), lambda i, m: (0, 0)) for _ in range(2 * groups)]
    in_specs += [pl.BlockSpec((tile, columns), lambda i, m, k=k: ((m[0] ^ k) * 2 + i, 0)) for k in (2, 0, 2, 0)]
    out = pl.BlockSpec((groups, tokens, tile), lambda i, m: (0, 0, i))
    return pl.pallas_call(
        input_grad_kernel,
        grid_spec=pltpu.PrefetchScalarGridSpec(
            num_scalar_prefetch=1, grid=(share // tile,), in_specs=in_specs, out_specs=[out, out]
        ),
        out_shape=[jax.ShapeDtypeStruct((groups, tokens, share), t) for t in (jnp.bfloat16, kept)],
        compiler_params=PARAMS,
        cost_estimate=LIGHT,
    )(jnp.reshape(m, (1,)).astype(jnp.int32), *owns, *others, weights, weights, other_weights, other_weights)


def chosen_kernel(flag, here_ref, there_ref, a_ref, b_ref):
    @pl.when(flag[0] == 1)
    def _():
        a_ref[...] = here_ref[...]
        b_ref[...] = there_ref[...]

    @pl.when(flag[0] == 0)
    def _():
        a_ref[...] = there_ref[...]
        b_ref[...] = here_ref[...]


def chosen(flag, run, here, there, runs):
    tokens, width = there.shape
    width = width // runs
    block = (tokens // 2, width)
    return pl.pallas_call(
        chosen_kernel,
        grid_spec=pltpu.PrefetchScalarGridSpec(
            num_scalar_prefetch=1,
            grid=(2,),
            in_specs=[pl.BlockSpec(block, lambda i, flag: (i, flag[1]))] * 2,
            out_specs=[pl.BlockSpec(block, lambda i, flag: (i, 0))] * 2,
        ),
        out_shape=[jax.ShapeDtypeStruct((tokens, width), here.dtype)] * 2,
        compiler_params=PARAMS,
        cost_estimate=LIGHT,
    )(jnp.stack([flag.astype(jnp.int32), run.astype(jnp.int32)]), here, there)


def summed_kernel(a_ref, b_ref, out_ref):
    out_ref[...] = (a_ref[...].astype(jnp.float32) + b_ref[...].astype(jnp.float32)).astype(out_ref.dtype)


def summed(a, b):
    block = pl.BlockSpec((1, *a.shape[1:]), lambda i: (i, 0, 0))
    return pl.pallas_call(
        summed_kernel,
        grid=(a.shape[0],),
        in_specs=[block, block],
        out_specs=block,
        out_shape=jax.ShapeDtypeStruct(a.shape, jnp.bfloat16),
        compiler_params=PARAMS,
        cost_estimate=LIGHT,
    )(a, b)


def weight_grad_kernel(at, *refs):
    lefts, grads_ref = refs[:4], refs[4]
    mantissa_ref, scale_ref = refs[-2:]
    top = total = None
    for i, left in enumerate(lefts):
        part = jnp.dot(grads_ref[i], left[...], preferred_element_type=jnp.float32)
        total = part if total is None else total + part
        top = jnp.abs(part) if top is None else jnp.maximum(top, jnp.abs(part))
    columns, rows = top.shape
    blocks = columns // BLOCK
    scale = jnp.max(top.reshape(blocks, BLOCK, rows), axis=1) + 1e-6
    for k in range(2):
        scale_ref[k] = scale[k * (blocks // 2) : (k + 1) * (blocks // 2)]
    inverse = 1.0 / scale
    scaled = [
        (total[b * BLOCK : (b + 1) * BLOCK] * inverse[b : b + 1]).astype(jnp.bfloat16) for b in range(blocks)
    ]
    half = blocks // 2
    mantissa_ref[:, 0, :] = jnp.concatenate(scaled[:half], axis=0).T
    mantissa_ref[:, 1, :] = jnp.concatenate(scaled[half:], axis=0).T


def weight_grad(at, lefts, grads, into, row_total):
    columns = grads.shape[1]
    tokens, rows = lefts[0].shape
    in_specs = [pl.BlockSpec((tokens, TILE), lambda i, at: (0, i)) for _ in lefts]
    in_specs.append(pl.BlockSpec(grads.shape, lambda i, at: (0, 0, 0)))
    operands = [*lefts, grads]
    aliases = {}
    for n, held in enumerate(into):
        in_specs.append(pl.BlockSpec(memory_space=pl.ANY))
        operands.append(held)
        aliases[len(operands)] = n
    return pl.pallas_call(
        weight_grad_kernel,
        grid_spec=pltpu.PrefetchScalarGridSpec(
            num_scalar_prefetch=1,
            grid=(rows // TILE,),
            in_specs=in_specs,
            out_specs=[
                pl.BlockSpec((TILE, 2, columns // 2), lambda i, at: (at[0] + i, 0, 0)),
                pl.BlockSpec((2, columns // BLOCK // 2, TILE), lambda i, at: (0, 0, at[0] + i)),
            ],
        ),
        out_shape=[
            jax.ShapeDtypeStruct((row_total, 2, columns // 2), jnp.bfloat16),
            jax.ShapeDtypeStruct((2, columns // BLOCK // 2, row_total), jnp.float32),
        ],
        input_output_aliases=aliases,
        compiler_params=PARAMS,
        cost_estimate=LIGHT,
    )(at, *operands)


def rows_placed_kernel(at, mantissa_ref, scale_ref, held_m, held_s, out_m_ref, out_s_ref):
    out_m_ref[...] = mantissa_ref[...]
    out_s_ref[...] = scale_ref[...]


def rows_placed(at, part, into):
    mantissa, scale = part
    rows, pair, columns = mantissa.shape
    tile = TILE
    blocks = scale.shape[1]
    return pl.pallas_call(
        rows_placed_kernel,
        grid_spec=pltpu.PrefetchScalarGridSpec(
            num_scalar_prefetch=1,
            grid=(rows // tile,),
            in_specs=[
                pl.BlockSpec((tile, pair, columns), lambda i, at: (i, 0, 0)),
                pl.BlockSpec((2, blocks, tile), lambda i, at: (0, 0, i)),
                pl.BlockSpec(memory_space=pl.ANY),
                pl.BlockSpec(memory_space=pl.ANY),
            ],
            out_specs=[
                pl.BlockSpec((tile, pair, columns), lambda i, at: (at[0] + i, 0, 0)),
                pl.BlockSpec((2, blocks, tile), lambda i, at: (0, 0, at[0] + i)),
            ],
        ),
        out_shape=[jax.ShapeDtypeStruct(held.shape, held.dtype) for held in into],
        input_output_aliases={3: 0, 4: 1},
        compiler_params=PARAMS,
        cost_estimate=LIGHT,
    )(at, mantissa, scale, *into)


def placed_kernel(group, *refs):
    terms, out_ref = refs[:-1], refs[-1]
    if len(terms) == 1:
        out_ref[...] = terms[0][0]
    else:
        out_ref[...] = (terms[0][0].astype(jnp.float32) + terms[1][0].astype(jnp.float32)).astype(jnp.bfloat16)


def placed_again_kernel(group, *refs):
    placed_kernel(group, *refs[:-2], refs[-1])


def placed(group, first, terms, into, groups):
    some, tokens, width = terms[0].shape
    in_specs = [pl.BlockSpec((1, tokens, width), lambda i, group: (i, 0, 0)) for _ in terms]
    operands = list(terms)
    aliases = {}
    if into is not None:
        in_specs.append(pl.BlockSpec(memory_space=pl.ANY))
        operands.append(into)
        aliases[len(operands)] = 0
    return pl.pallas_call(
        placed_kernel if into is None else placed_again_kernel,
        grid_spec=pltpu.PrefetchScalarGridSpec(
            num_scalar_prefetch=1,
            grid=(some,),
            in_specs=in_specs,
            out_specs=pl.BlockSpec((tokens, width), lambda i, group: (group[0] ^ (first + i), 0)),
        ),
        out_shape=jax.ShapeDtypeStruct((groups * tokens, width), jnp.bfloat16),
        input_output_aliases=aliases,
        compiler_params=PARAMS,
        cost_estimate=LIGHT,
    )(jnp.reshape(group, (1,)).astype(jnp.int32), *operands)


def on_device(layer_input, kv_cotangent, kv_weight):
    n_pipe, n_dp, n_mp = (lax.axis_size(a) for a in ("pipe", "dp", "mp"))
    p, m = lax.axis_index("dp"), lax.axis_index("mp")
    features = layer_input[0]
    tokens, width = features.shape
    columns = 2 * kv_cotangent.shape[3]
    rows = kv_weight.shape[1]
    share = rows // n_mp

    def move(x, where):
        pairs = []
        for s in range(n_pipe):
            for i in range(n_dp):
                for j in range(n_mp):
                    to = where(s, i, j)
                    if to is not None:
                        pairs.append(((s * n_dp + i) * n_mp + j, (to[0] * n_dp + to[1]) * n_mp + to[2]))
        return lax.ppermute(x, ("pipe", "dp", "mp"), pairs)

    def across(x):
        return move(x, lambda s, i, j: (s, i, j ^ 2))

    def other_core(x):
        return move(x, lambda s, i, j: (s, i, j ^ 1))

    def near(x, other):
        return move(x, lambda s, i, j: (s, 2 * (i // 2) + j % 2, 2 * (j // 2) + (i + other) % 2))

    def far(x, other):
        return move(x, lambda s, i, j: (s, 2 * (1 - i // 2) + j % 2, 2 * (j // 2) + (i + other) % 2))

    def across(x):
        return move(x, lambda s, i, j: (s, i, j ^ 2))

    def behind(x):
        return move(x, lambda s, i, j: (s - 1, i, j) if s else None)

    def behind_across(x):
        return move(x, lambda s, i, j: (s - 1, i, j ^ 2) if s else None)

    def across_but_first(x):
        return move(x, lambda s, i, j: (s, i, j ^ 2) if s else None)

    same = (m ^ p) & 1
    slots = jnp.where(same == 0, jnp.array([0, 1, 2, 3], jnp.int32), jnp.array([1, 0, 3, 2], jnp.int32))
    own_side = (m // 2) == (p // 2)
    half = width // 2
    run = half // 2
    core = m & 1
    direct_at = jnp.where(own_side, 0, half)
    crossed_at = jnp.where(own_side, half, 0)

    def tile_at(first):
        return jnp.reshape(first // TILE, (1,)).astype(jnp.int32)

    last = []

    def now(x):
        return lax.optimization_barrier((x, *last))[0] if last else x

    def ran(x):
        last[:] = [x]

    def step(x):
        x = now(x)
        ran(x)
        return x

    def group(k, x):
        return move(x, lambda s, i, j: (s, i ^ k, j))

    g0 = kv_cotangent[0].reshape(tokens, columns)
    own_w = step(kv_weight[0].reshape(rows, columns))
    other_raw = step(other_core(kv_weight))
    g0_core = step(other_core(g0))
    other_w = step(other_raw[0].reshape(rows, columns))
    g1 = step(group(1, g0))
    g2 = step(group(2, g0))
    g1_core = step(other_core(g1))
    a_early, m_early = input_grad(
        m, (now(g0), g1), (g0_core, g1_core), own_w, other_w, n_mp, jnp.float32
    )
    ran(a_early)
    there = step(across(features[:, half:]))
    near0_sent, far0_sent = chosen(own_side, p & 1, features, now(there), 2)
    ran(near0_sent)
    g3 = step(group(3, g0))
    near1_sent, far1_sent = chosen(own_side, (p + 1) & 1, features, now(there), 2)
    ran(near1_sent)
    g2_core = step(other_core(g2))
    near1_begun = near(now(near1_sent), 1)
    g3_core = step(other_core(g3))
    a_late, m_late = input_grad(
        m, (now(g2), g3), (g2_core, g3_core), own_w, other_w, n_mp, jnp.bfloat16
    )
    ran(a_late)
    far1_begun = far(now(far1_sent), 1)
    near0 = step(near(near0_sent, 0))
    near1 = step(near1_begun)
    near1_x_begun = across(now(near1))
    a_across = step(across_but_first(a_early))
    early_sum = step(summed(now(m_early), a_across))
    far0 = step(far(far0_sent, 0))
    other_turned = step(turned(slots, (now(g0_core), g1_core, g2_core, g3_core)))
    late_across_begun = behind_across(now(a_late))
    late_own = step(behind(m_late))
    own_turned = step(turned(slots, (now(g0), g1, g2, g3)))
    near0_x = step(across(near0))
    near1_x = step(near1_x_begun)
    far1 = step(far1_begun)
    far1_x_begun = across(now(far1))
    direct_m_sent, direct_s_sent = weight_grad(tile_at(0), (now(near0), near1, far0, far1), other_turned, (), run)
    ran(direct_m_sent)
    early_begun = behind(now(early_sum))
    out = weight_grad(tile_at(direct_at + core * run), (now(near0), near1, far0, far1), own_turned, (), rows)
    ran(out[0])
    late_across = step(late_across_begun)
    total = step(placed(p, 2, (now(late_own), late_across), None, n_dp))
    far0_x = step(across(far0))
    far1_x = step(far1_x_begun)
    crossed_m_sent, crossed_s_sent = weight_grad(tile_at(0), (now(near0_x), near1_x, far0_x, far1_x), other_turned, (), run)
    ran(crossed_m_sent)
    out = weight_grad(tile_at(crossed_at + core * run), (now(near0_x), near1_x, far0_x, far1_x), own_turned, out, rows)
    ran(out[0])
    direct_m = step(other_core(direct_m_sent))
    direct_s = step(other_core(direct_s_sent))
    out = rows_placed(tile_at(direct_at + (1 - core) * run), (now(direct_m), direct_s), out)
    ran(out[0])
    early = step(early_begun)
    total = step(placed(p, 0, (now(early),), total, n_dp))
    crossed_m = step(other_core(crossed_m_sent))
    crossed_s = step(other_core(crossed_s_sent))
    out = rows_placed(tile_at(crossed_at + (1 - core) * run), (now(crossed_m), crossed_s), out)
    ran(out[0])
    mantissa, scale = out
    scale = scale.transpose(2, 0, 1)
    return (total[None], mantissa[None], scale[None])


def solution(mesh):
    in_specs = (P("pipe", "dp", "mp"), P("pipe", "dp", None, "mp"), P("pipe", "dp", None, "mp"))
    out_specs = (
        P("pipe", None, ("dp", "mp")),
        P("pipe", "dp", None, "mp"),
        P("pipe", "dp", None, "mp"),
    )
    return jax.shard_map(on_device, mesh=mesh, in_specs=in_specs, out_specs=out_specs, check_vma=False)
```

```python
import jax
import jax.numpy as jnp
from jax import lax
from jax.experimental import pallas as pl
from jax.experimental.pallas import tpu as pltpu
from jax.sharding import PartitionSpec as P

BLOCK = 128
TILE = 512
MIB = 1024 * 1024
VMEM_MIB = 60
PARAMS = pltpu.CompilerParams(vmem_limit_bytes=VMEM_MIB * MIB)
LIGHT = pl.CostEstimate(flops=0, bytes_accessed=0, transcendentals=0)


def turned_kernel(slots, *refs):
    for k, ref in enumerate(refs[:-1]):
        refs[-1][slots[k]] = ref[...].T


def turned(slots, grads):
    tokens, columns = grads[0].shape
    return pl.pallas_call(
        turned_kernel,
        grid_spec=pltpu.PrefetchScalarGridSpec(
            num_scalar_prefetch=1,
            grid=(1,),
            in_specs=[pl.BlockSpec((tokens, columns), lambda i, slots: (0, 0)) for _ in grads],
            out_specs=pl.BlockSpec((4, columns, tokens), lambda i, slots: (0, 0, 0)),
        ),
        out_shape=jax.ShapeDtypeStruct((4, columns, tokens), jnp.bfloat16),
        compiler_params=PARAMS,
        cost_estimate=LIGHT,
    )(slots, *grads)


def across_dot(a, b):
    return lax.dot_general(a, b, (((1,), (1,)), ((), ())), preferred_element_type=jnp.float32)


def input_grad_kernel(m, *refs):
    groups = (len(refs) - 6) // 2
    owns, others = refs[:groups], refs[groups : 2 * groups]
    own2_ref, own0_ref, other2_ref, other0_ref, a_ref, m_ref = refs[2 * groups :]
    for n in range(groups):
        own, other = owns[n][...], others[n][...]
        a = across_dot(own, own2_ref[...]) + across_dot(other, other2_ref[...])
        a_ref[n] = a.astype(a_ref.dtype)
        b = across_dot(own, own0_ref[...]) + across_dot(other, other0_ref[...])
        m_ref[n] = b.astype(m_ref.dtype)


def input_grad(m, owns, others, weights, other_weights, parts, kept):
    tokens, columns = owns[0].shape
    groups = len(owns)
    share = weights.shape[0] // parts
    tile = share // 2
    in_specs = [pl.BlockSpec((tokens, columns), lambda i, m: (0, 0)) for _ in range(2 * groups)]
    in_specs += [pl.BlockSpec((tile, columns), lambda i, m, k=k: ((m[0] ^ k) * 2 + i, 0)) for k in (2, 0, 2, 0)]
    out = pl.BlockSpec((groups, tokens, tile), lambda i, m: (0, 0, i))
    return pl.pallas_call(
        input_grad_kernel,
        grid_spec=pltpu.PrefetchScalarGridSpec(
            num_scalar_prefetch=1, grid=(share // tile,), in_specs=in_specs, out_specs=[out, out]
        ),
        out_shape=[jax.ShapeDtypeStruct((groups, tokens, share), t) for t in (jnp.bfloat16, kept)],
        compiler_params=PARAMS,
        cost_estimate=LIGHT,
    )(jnp.reshape(m, (1,)).astype(jnp.int32), *owns, *others, weights, weights, other_weights, other_weights)


def chosen_kernel(flag, here_ref, there_ref, a_ref, b_ref):
    @pl.when(flag[0] == 1)
    def _():
        a_ref[...] = here_ref[...]
        b_ref[...] = there_ref[...]

    @pl.when(flag[0] == 0)
    def _():
        a_ref[...] = there_ref[...]
        b_ref[...] = here_ref[...]


def chosen(flag, run, here, there, runs):
    tokens, width = there.shape
    width = width // runs
    block = (tokens // 2, width)
    return pl.pallas_call(
        chosen_kernel,
        grid_spec=pltpu.PrefetchScalarGridSpec(
            num_scalar_prefetch=1,
            grid=(2,),
            in_specs=[pl.BlockSpec(block, lambda i, flag: (i, flag[1]))] * 2,
            out_specs=[pl.BlockSpec(block, lambda i, flag: (i, 0))] * 2,
        ),
        out_shape=[jax.ShapeDtypeStruct((tokens, width), here.dtype)] * 2,
        compiler_params=PARAMS,
        cost_estimate=LIGHT,
    )(jnp.stack([flag.astype(jnp.int32), run.astype(jnp.int32)]), here, there)


def summed_kernel(a_ref, b_ref, out_ref):
    out_ref[...] = (a_ref[...].astype(jnp.float32) + b_ref[...].astype(jnp.float32)).astype(out_ref.dtype)


def summed(a, b):
    block = pl.BlockSpec((1, *a.shape[1:]), lambda i: (i, 0, 0))
    return pl.pallas_call(
        summed_kernel,
        grid=(a.shape[0],),
        in_specs=[block, block],
        out_specs=block,
        out_shape=jax.ShapeDtypeStruct(a.shape, jnp.bfloat16),
        compiler_params=PARAMS,
        cost_estimate=LIGHT,
    )(a, b)


def weight_grad_kernel(at, *refs):
    lefts, grads_ref = refs[:4], refs[4]
    mantissa_ref, scale_ref = refs[-2:]
    top = total = None
    for i, left in enumerate(lefts):
        part = jnp.dot(grads_ref[i], left[...], preferred_element_type=jnp.float32)
        total = part if total is None else total + part
        top = jnp.abs(part) if top is None else jnp.maximum(top, jnp.abs(part))
    columns, rows = top.shape
    blocks = columns // BLOCK
    scale = jnp.max(top.reshape(blocks, BLOCK, rows), axis=1) + 1e-6
    for k in range(2):
        scale_ref[k] = scale[k * (blocks // 2) : (k + 1) * (blocks // 2)]
    inverse = 1.0 / scale
    scaled = [
        (total[b * BLOCK : (b + 1) * BLOCK] * inverse[b : b + 1]).astype(jnp.bfloat16) for b in range(blocks)
    ]
    half = blocks // 2
    mantissa_ref[:, 0, :] = jnp.concatenate(scaled[:half], axis=0).T
    mantissa_ref[:, 1, :] = jnp.concatenate(scaled[half:], axis=0).T


def weight_grad(at, lefts, grads, into, row_total):
    columns = grads.shape[1]
    tokens, rows = lefts[0].shape
    in_specs = [pl.BlockSpec((tokens, TILE), lambda i, at: (0, i)) for _ in lefts]
    in_specs.append(pl.BlockSpec(grads.shape, lambda i, at: (0, 0, 0)))
    operands = [*lefts, grads]
    aliases = {}
    for n, held in enumerate(into):
        in_specs.append(pl.BlockSpec(memory_space=pl.ANY))
        operands.append(held)
        aliases[len(operands)] = n
    return pl.pallas_call(
        weight_grad_kernel,
        grid_spec=pltpu.PrefetchScalarGridSpec(
            num_scalar_prefetch=1,
            grid=(rows // TILE,),
            in_specs=in_specs,
            out_specs=[
                pl.BlockSpec((TILE, 2, columns // 2), lambda i, at: (at[0] + i, 0, 0)),
                pl.BlockSpec((2, columns // BLOCK // 2, TILE), lambda i, at: (0, 0, at[0] + i)),
            ],
        ),
        out_shape=[
            jax.ShapeDtypeStruct((row_total, 2, columns // 2), jnp.bfloat16),
            jax.ShapeDtypeStruct((2, columns // BLOCK // 2, row_total), jnp.float32),
        ],
        input_output_aliases=aliases,
        compiler_params=PARAMS,
        cost_estimate=LIGHT,
    )(at, *operands)


def rows_placed_kernel(at, mantissa_ref, scale_ref, held_m, held_s, out_m_ref, out_s_ref):
    out_m_ref[...] = mantissa_ref[...]
    out_s_ref[...] = scale_ref[...]


def rows_placed(at, part, into):
    mantissa, scale = part
    rows, pair, columns = mantissa.shape
    tile = TILE
    blocks = scale.shape[1]
    return pl.pallas_call(
        rows_placed_kernel,
        grid_spec=pltpu.PrefetchScalarGridSpec(
            num_scalar_prefetch=1,
            grid=(rows // tile,),
            in_specs=[
                pl.BlockSpec((tile, pair, columns), lambda i, at: (i, 0, 0)),
                pl.BlockSpec((2, blocks, tile), lambda i, at: (0, 0, i)),
                pl.BlockSpec(memory_space=pl.ANY),
                pl.BlockSpec(memory_space=pl.ANY),
            ],
            out_specs=[
                pl.BlockSpec((tile, pair, columns), lambda i, at: (at[0] + i, 0, 0)),
                pl.BlockSpec((2, blocks, tile), lambda i, at: (0, 0, at[0] + i)),
            ],
        ),
        out_shape=[jax.ShapeDtypeStruct(held.shape, held.dtype) for held in into],
        input_output_aliases={3: 0, 4: 1},
        compiler_params=PARAMS,
        cost_estimate=LIGHT,
    )(at, mantissa, scale, *into)


def placed_kernel(group, *refs):
    terms, out_ref = refs[:-1], refs[-1]
    if len(terms) == 1:
        out_ref[...] = terms[0][0]
    else:
        out_ref[...] = (terms[0][0].astype(jnp.float32) + terms[1][0].astype(jnp.float32)).astype(jnp.bfloat16)


def placed_again_kernel(group, *refs):
    placed_kernel(group, *refs[:-2], refs[-1])


def placed(group, first, terms, into, groups):
    some, tokens, width = terms[0].shape
    in_specs = [pl.BlockSpec((1, tokens, width), lambda i, group: (i, 0, 0)) for _ in terms]
    operands = list(terms)
    aliases = {}
    if into is not None:
        in_specs.append(pl.BlockSpec(memory_space=pl.ANY))
        operands.append(into)
        aliases[len(operands)] = 0
    return pl.pallas_call(
        placed_kernel if into is None else placed_again_kernel,
        grid_spec=pltpu.PrefetchScalarGridSpec(
            num_scalar_prefetch=1,
            grid=(some,),
            in_specs=in_specs,
            out_specs=pl.BlockSpec((tokens, width), lambda i, group: (group[0] ^ (first + i), 0)),
        ),
        out_shape=jax.ShapeDtypeStruct((groups * tokens, width), jnp.bfloat16),
        input_output_aliases=aliases,
        compiler_params=PARAMS,
        cost_estimate=LIGHT,
    )(jnp.reshape(group, (1,)).astype(jnp.int32), *operands)


def on_device(layer_input, kv_cotangent, kv_weight):
    n_pipe, n_dp, n_mp = (lax.axis_size(a) for a in ("pipe", "dp", "mp"))
    p, m = lax.axis_index("dp"), lax.axis_index("mp")
    features = layer_input[0]
    tokens, width = features.shape
    columns = 2 * kv_cotangent.shape[3]
    rows = kv_weight.shape[1]
    share = rows // n_mp

    def move(x, where):
        pairs = []
        for s in range(n_pipe):
            for i in range(n_dp):
                for j in range(n_mp):
                    to = where(s, i, j)
                    if to is not None:
                        pairs.append(((s * n_dp + i) * n_mp + j, (to[0] * n_dp + to[1]) * n_mp + to[2]))
        return lax.ppermute(x, ("pipe", "dp", "mp"), pairs)

    def across(x):
        return move(x, lambda s, i, j: (s, i, j ^ 2))

    def other_core(x):
        return move(x, lambda s, i, j: (s, i, j ^ 1))

    def near(x, other):
        return move(x, lambda s, i, j: (s, 2 * (i // 2) + j % 2, 2 * (j // 2) + (i + other) % 2))

    def far(x, other):
        return move(x, lambda s, i, j: (s, 2 * (1 - i // 2) + j % 2, 2 * (j // 2) + (i + other) % 2))

    def across(x):
        return move(x, lambda s, i, j: (s, i, j ^ 2))

    def behind(x):
        return move(x, lambda s, i, j: (s - 1, i, j) if s else None)

    def behind_across(x):
        return move(x, lambda s, i, j: (s - 1, i, j ^ 2) if s else None)

    def across_but_first(x):
        return move(x, lambda s, i, j: (s, i, j ^ 2) if s else None)

    same = (m ^ p) & 1
    slots = jnp.where(same == 0, jnp.array([0, 1, 2, 3], jnp.int32), jnp.array([1, 0, 3, 2], jnp.int32))
    own_side = (m // 2) == (p // 2)
    half = width // 2
    run = half // 2
    core = m & 1
    direct_at = jnp.where(own_side, 0, half)
    crossed_at = jnp.where(own_side, half, 0)

    def tile_at(first):
        return jnp.reshape(first // TILE, (1,)).astype(jnp.int32)

    last = []

    def now(x):
        return lax.optimization_barrier((x, *last))[0] if last else x

    def ran(x):
        last[:] = [x]

    def step(x):
        x = now(x)
        ran(x)
        return x

    def group(k, x):
        return move(x, lambda s, i, j: (s, i ^ k, j))

    g0 = kv_cotangent[0].reshape(tokens, columns)
    own_w = step(kv_weight[0].reshape(rows, columns))
    other_raw = step(other_core(kv_weight))
    g0_core = step(other_core(g0))
    other_w = step(other_raw[0].reshape(rows, columns))
    g1 = step(group(1, g0))
    g2 = step(group(2, g0))
    g1_core = step(other_core(g1))
    a_early, m_early = input_grad(
        m, (now(g0), g1), (g0_core, g1_core), own_w, other_w, n_mp, jnp.float32
    )
    ran(a_early)
    there = step(across(features[:, half:]))
    near0_sent, far0_sent = chosen(own_side, p & 1, features, now(there), 2)
    ran(near0_sent)
    g3 = step(group(3, g0))
    near1_sent, far1_sent = chosen(own_side, (p + 1) & 1, features, now(there), 2)
    ran(near1_sent)
    g2_core = step(other_core(g2))
    near1_begun = near(now(near1_sent), 1)
    g3_core = step(other_core(g3))
    a_late, m_late = input_grad(
        m, (now(g2), g3), (g2_core, g3_core), own_w, other_w, n_mp, jnp.bfloat16
    )
    ran(a_late)
    far1_begun = far(now(far1_sent), 1)
    near0 = step(near(near0_sent, 0))
    near1 = step(near1_begun)
    near1_x_begun = across(now(near1))
    a_across = step(across_but_first(a_early))
    early_sum = step(summed(now(m_early), a_across))
    far0 = step(far(far0_sent, 0))
    late_across_begun = behind_across(now(a_late))
    late_own = step(behind(m_late))
    other_turned = step(turned(slots, (now(g0_core), g1_core, g2_core, g3_core)))
    own_turned = step(turned(slots, (now(g0), g1, g2, g3)))
    near0_x = step(across(near0))
    near1_x = step(near1_x_begun)
    far1 = step(far1_begun)
    far1_x_begun = across(now(far1))
    direct_m_sent, direct_s_sent = weight_grad(tile_at(0), (now(near0), near1, far0, far1), other_turned, (), run)
    ran(direct_m_sent)
    early_begun = behind(now(early_sum))
    out = weight_grad(tile_at(direct_at + core * run), (now(near0), near1, far0, far1), own_turned, (), rows)
    ran(out[0])
    far0_x = step(across(far0))
    late_across = step(late_across_begun)
    total = step(placed(p, 2, (now(late_own), late_across), None, n_dp))
    far1_x = step(far1_x_begun)
    crossed_m_sent, crossed_s_sent = weight_grad(tile_at(0), (now(near0_x), near1_x, far0_x, far1_x), other_turned, (), run)
    ran(crossed_m_sent)
    out = weight_grad(tile_at(crossed_at + core * run), (now(near0_x), near1_x, far0_x, far1_x), own_turned, out, rows)
    ran(out[0])
    direct_m = step(other_core(direct_m_sent))
    direct_s = step(other_core(direct_s_sent))
    out = rows_placed(tile_at(direct_at + (1 - core) * run), (now(direct_m), direct_s), out)
    ran(out[0])
    early = step(early_begun)
    total = step(placed(p, 0, (now(early),), total, n_dp))
    crossed_m = step(other_core(crossed_m_sent))
    crossed_s = step(other_core(crossed_s_sent))
    out = rows_placed(tile_at(crossed_at + (1 - core) * run), (now(crossed_m), crossed_s), out)
    ran(out[0])
    mantissa, scale = out
    scale = scale.transpose(2, 0, 1)
    return (total[None], mantissa[None], scale[None])


def solution(mesh):
    in_specs = (P("pipe", "dp", "mp"), P("pipe", "dp", None, "mp"), P("pipe", "dp", None, "mp"))
    out_specs = (
        P("pipe", None, ("dp", "mp")),
        P("pipe", "dp", None, "mp"),
        P("pipe", "dp", None, "mp"),
    )
    return jax.shard_map(on_device, mesh=mesh, in_specs=in_specs, out_specs=out_specs, check_vma=False)
```
